32 devices in a mesh: row: 8 (over y, x, core), col: 4 (over z).
Axes of the slice: x: 2, y: 2, z: 4, core: 2. Of those that a mesh axis runs over, the one named last changes fastest.
Arguments:
- matrix: float32 [4096, 4096], P('row', 'col'), may hold values from -50 to 50
- panel_index: int32 [1], replicated, may hold values from 0 to 14
Outputs:
- factored: float32 [4096, 4096], P('row', 'col')
The draws below stay inside these ranges and needn't reach their ends.
All inputs are finite; a program needn't handle non-finite values.
Results may differ from the reference program's by a relative error of at most 0.0003.
Values sent between devices are 32-bit elements; how exact they have to be, the bound alone decides.
A program may use at most 64 MiB of HBM per device.

```python
import math
import jax
import jax.numpy as jnp
from jax import lax

NB = 128
BLK_DEV = 8
STEPS = 2
ROWS = 4096
BLOCKS = 32
COLS = 4096
N_COL = 4


def draw_matrix(key, part):
    key = jax.random.fold_in(key, 11)
    key_base, key_rows, key_cols = jax.random.split(key, 3)
    row_scale = jnp.exp(jax.random.uniform(key_rows, (ROWS, 1), jnp.float32, math.log(0.5), math.log(5.0)))
    col_scale = jnp.exp(jax.random.uniform(key_cols, (1, COLS), jnp.float32, math.log(0.5), math.log(2.0)))
    base_draw = jnp.clip(jax.random.normal(key_base, (ROWS, COLS), jnp.float32), -5.0, 5.0)
    values = base_draw * row_scale * col_scale
    return values.astype(jnp.float32)


def setup_inputs(seed: int = 0) -> dict:
    arg_keys = jax.random.split(jax.random.key(seed), 3)
    matrix = draw_matrix(jax.random.fold_in(arg_keys[2], 71), 0)
    panel_index = jax.random.randint(arg_keys[1], (1,), 0, BLOCKS // 2 - STEPS + 1).astype(jnp.int32)
    return dict(matrix=matrix, panel_index=panel_index)


HIGHEST_PRECISION = lax.Precision.HIGHEST

def triangular_solve_left(coef_matrix, right_matrix, lower, unit_diag):
    return lax.linalg.triangular_solve(coef_matrix, right_matrix, left_side=True, lower=lower, unit_diagonal=unit_diag)

def triangular_split(square):
    order_size = square.shape[0]
    positions = jnp.arange(order_size, dtype=jnp.int32)
    identity = jnp.eye(order_size, dtype=square.dtype)

    def eliminate(column_index, carry):
        remaining, lower_unit = carry
        pivot_row = remaining[column_index]
        pivot_value = pivot_row[column_index]
        multiplier = jnp.where(positions > column_index, remaining[:, column_index] / pivot_value, jnp.zeros((), square.dtype))
        remaining = remaining - multiplier[:, None] * pivot_row[None, :]
        lower_unit = lower_unit + multiplier[:, None] * (positions[None, :] == column_index).astype(square.dtype)
        return (remaining, lower_unit)
    remaining, lower_unit = lax.fori_loop(0, order_size, eliminate, (square, identity))
    return (lower_unit, jnp.triu(remaining))

def reference(matrix, panel_index):
    row_count, col_count = matrix.shape
    dtype_used = matrix.dtype
    identity = jnp.eye(NB, dtype=dtype_used)
    stored_block = jnp.arange(col_count, dtype=jnp.int32) // NB
    column_block = stored_block % BLK_DEV * N_COL + stored_block // BLK_DEV
    global_row = jnp.arange(row_count, dtype=jnp.int32)
    diag_index = jnp.arange(NB, dtype=jnp.int32)
    current = matrix
    for section_index in range(STEPS):
        target = (panel_index[0] + section_index).astype(jnp.int32)
        stored_start = ((target % N_COL * BLK_DEV + target // N_COL) * NB).astype(jnp.int32)
        first_row = (target * NB).astype(jnp.int32)
        active = global_row >= first_row
        initial = lax.dynamic_slice_in_dim(current, stored_start, NB, 1)
        panel_block = jnp.where(active[:, None], initial, jnp.zeros((), dtype_used))
        ortho_full, tri_factor = jnp.linalg.qr(panel_block)
        sign_fix = jnp.where(jnp.diagonal(tri_factor) < 0, -1.0, 1.0).astype(dtype_used)
        ortho_full = ortho_full * sign_fix[None, :]
        shift_rows = ((global_row - first_row)[:, None] == diag_index[None, :]).astype(dtype_used)
        shifted = ortho_full + shift_rows
        top_block = lax.dynamic_slice_in_dim(shifted, first_row, NB, 0)
        lower_unit, upper_tri = triangular_split(top_block)
        upper_inv = triangular_solve_left(upper_tri, identity, False, False)
        reflect = jnp.dot(shifted, upper_inv, precision=HIGHEST_PRECISION)
        reflect = jnp.where(active[:, None], reflect, jnp.zeros((), dtype_used))
        t_transposed = triangular_solve_left(lower_unit, upper_tri.T, True, True)
        projection = jnp.dot(reflect.T, current, precision=HIGHEST_PRECISION)
        coefficients = jnp.dot(t_transposed, projection, precision=HIGHEST_PRECISION)
        change = jnp.dot(reflect, coefficients, precision=HIGHEST_PRECISION)
        trailing = column_block > target
        current = jnp.where(trailing[None, :], current - change, current)
        new_panel = jnp.where(active[:, None], reflect, initial)
        current = lax.dynamic_update_slice_in_dim(current, new_panel, stored_start, 1)
    return current
```

```python
import jax
import jax.numpy as jnp
from jax import lax
from jax.experimental import pallas as pl
from jax.experimental.pallas import tpu as pltpu
from jax.sharding import PartitionSpec as P

NB = 128
SUB = 32
HI = lax.Precision.HIGHEST


def mm(a, b, ca=1, cb=0):
    return lax.dot_general(
        a, b, (((ca,), (cb,)), ((), ())), precision=HI, preferred_element_type=jnp.float32
    )


def eliminate(chains, m_ref, n_ref):
    count = len(chains)
    rows = lax.broadcasted_iota(jnp.int32, (NB, NB), 0)
    cols = lax.broadcasted_iota(jnp.int32, (NB, NB), 1)
    unit = (rows == cols).astype(jnp.float32)
    sub_row = lax.broadcasted_iota(jnp.int32, (SUB, 1), 0)
    for i, a in enumerate(chains):
        m_ref[i] = a
        n_ref[i] = unit
    pivots = [[] for _ in chains]
    for start in range(0, NB, SUB):
        m = [m_ref[i, start : start + SUB, :] for i in range(count)]
        n = [n_ref[i, start : start + SUB, :] for i in range(count)]
        inv = [jnp.zeros((SUB, 1), jnp.float32) for _ in range(count)]
        for j in range(SUB):
            c = start + j
            for i in range(count):
                recip = 1.0 / m[i][j : j + 1, c : c + 1]
                inv[i] = jnp.where(sub_row == j, recip, inv[i])
                if j < SUB - 1:
                    mult = jnp.where(sub_row > j, m[i][:, c : c + 1] * recip, 0.0)
                    m[i] = m[i] - mult * m[i][j : j + 1, :]
                    n[i] = n[i] - mult * n[i][j : j + 1, :]
        for i in range(count):
            n_ref[i, start : start + SUB, :] = n[i]
            pivots[i].append(inv[i])
        rest = start + SUB
        if rest < NB:
            for i in range(count):
                other = m[count - 1 - i] * inv[count - 1 - i]
                both = jnp.concatenate([m[i], n[i]], axis=1)
                change = mm(other, both, 0, 0)
                m_ref[i, rest:, :] -= change[rest:, :NB]
                n_ref[i, rest:, :] -= change[rest:, NB:]
    return [jnp.concatenate(p, axis=0) for p in pivots]


def factor_panel(gram, top, m_ref, n_ref):
    rows = lax.broadcasted_iota(jnp.int32, (NB, NB), 0)
    cols = lax.broadcasted_iota(jnp.int32, (NB, NB), 1)
    unit = (rows == cols).astype(jnp.float32)
    (inv,) = eliminate([gram], m_ref, n_ref)
    w = n_ref[0] * jnp.sqrt(inv)
    b = mm(top, w, 1, 1) + unit
    _, inv_t = eliminate([b, b.T], m_ref, n_ref)
    v = n_ref[1] * inv_t
    k = mm(v, n_ref[0], 0, 0)
    return w, b, k, v


def factor_kernel(small_ref, out_ref, m_ref, n_ref):
    g11 = small_ref[0:NB, 0:NB]
    g12 = small_ref[0:NB, NB:]
    g22 = small_ref[NB : 2 * NB, NB:]
    t11 = small_ref[2 * NB : 3 * NB, 0:NB]
    t12 = small_ref[2 * NB : 3 * NB, NB:]
    t21 = small_ref[3 * NB :, 0:NB]
    t22 = small_ref[3 * NB :, NB:]
    w1, b1, k1, v1 = factor_panel(g11 + mm(t11, t11, 0, 0), t11, m_ref, n_ref)
    x12 = mm(k1, mm(w1, g12) + mm(b1, t12, 0, 0))
    z = mm(w1, x12, 0, 0)
    g11z = mm(g11, z)
    zg = mm(z, g12, 0, 0)
    gram2 = g22 - zg - zg.T + mm(z, g11z, 0, 0)
    w2, b2, k2, v2 = factor_panel(gram2, t22 - mm(t21, z), m_ref, n_ref)
    for i, a in enumerate((w1, b1, k1, v1, z, w2, k2, v2, g12 - g11z, t21)):
        out_ref[i] = a


def finish_kernel(s_ref, c_ref, a_ref, bulk_ref, fac_ref, out_ref):
    row_off = s_ref[0]
    place1, place2, target, my_col, col_devices = s_ref[1], s_ref[2], s_ref[3], s_ref[4], s_ref[5]
    height, width = c_ref.shape
    rel = lax.broadcasted_iota(jnp.int32, (height, NB), 0) + row_off
    diag = lax.broadcasted_iota(jnp.int32, (height, NB), 1)
    w1, b1, k1, v1, z, w2, k2, v2, h, t21 = [fac_ref[i] for i in range(10)]
    p1 = jnp.where(rel >= 0, a_ref[:, 0:NB], 0.0)
    full1 = mm(p1, w1, 1, 1) + (rel == diag).astype(jnp.float32)
    p2 = jnp.where(rel >= NB, a_ref[:, NB:] - mm(p1, z), 0.0)
    full2 = mm(p2, w2, 1, 1) + (rel == diag + NB).astype(jnp.float32)
    y1 = mm(full1, v1, 1, 1)
    y2 = mm(full2, v2, 1, 1)
    both = jnp.concatenate([full1, full2], axis=1)
    step = 2 * NB

    def column(i, _):
        at = pl.ds(pl.multiple_of(i * step, step), step)
        s1 = bulk_ref[0:NB, at]
        s2 = bulk_ref[NB : 2 * NB, at]
        top1 = bulk_ref[2 * NB : 3 * NB, at]
        top2 = bulk_ref[3 * NB :, at]
        block = (
            lax.broadcasted_iota(jnp.int32, (NB, step), 1) // NB + i * (step // NB)
        ) * col_devices + my_col
        x1 = mm(k1, mm(w1, s1) + mm(b1, top1, 0, 0))
        u1 = mm(w1, x1, 0, 0)
        x2 = mm(w2, s2 - mm(z, s1, 0, 0) - mm(h, u1, 0, 0)) + top2 - mm(t21, u1)
        x2 = mm(k2, x2)
        x1 = jnp.where(block > target, x1, 0.0)
        x2 = jnp.where(block > target + 1, x2, 0.0)
        out_ref[:, at] = c_ref[:, at] - mm(both, jnp.concatenate([x1, x2], axis=0))
        return 0

    lax.fori_loop(0, width // step, column, 0)

    @pl.when(place1 >= 0)
    def _():
        at = pl.ds(pl.multiple_of(place1 * NB, NB), NB)
        out_ref[:, at] = jnp.where(rel >= 0, y1, out_ref[:, at])

    @pl.when(place2 >= 0)
    def _():
        at = pl.ds(pl.multiple_of(place2 * NB, NB), NB)
        out_ref[:, at] = jnp.where(rel >= NB, y2, out_ref[:, at])


def per_device(matrix, panel_index):
    height, width = matrix.shape
    col_devices = lax.axis_size("col")
    my_row = lax.axis_index("row")
    my_col = lax.axis_index("col")
    target = panel_index[0]
    first = target * NB
    second = first + NB
    global_row = my_row * height + jnp.arange(height, dtype=jnp.int32)

    def panel(which):
        block = lax.dynamic_slice_in_dim(matrix, which // col_devices * NB, NB, 1)
        return jnp.where(which % col_devices == my_col, block, 0.0)

    slab = lax.psum(jnp.concatenate([panel(target), panel(target + 1)], axis=1), "col")

    def top_rows(array):
        parts = []
        for at in (first, second):
            rows = lax.dynamic_slice_in_dim(array, at % height, NB, 0)
            parts.append(jnp.where(at // height == my_row, rows, 0.0))
        return parts

    below = jnp.where((global_row >= second)[:, None], slab, 0.0)
    gram = lax.dot_general(below, below, (((0,), (0,)), ((), ())), precision=HI)
    small = lax.psum(jnp.concatenate([gram] + top_rows(slab), axis=0), "row")
    product = lax.dot_general(below, matrix, (((0,), (0,)), ((), ())), precision=HI)
    bulk = jnp.concatenate([product] + top_rows(matrix), axis=0)
    bulk, small = lax.optimization_barrier((bulk, small))
    bulk = lax.psum(bulk, "row")
    factors = pl.pallas_call(
        factor_kernel,
        out_shape=jax.ShapeDtypeStruct((10, NB, NB), jnp.float32),
        in_specs=[pl.BlockSpec(memory_space=pltpu.VMEM)],
        out_specs=pl.BlockSpec(memory_space=pltpu.VMEM),
        scratch_shapes=[pltpu.VMEM((2, NB, NB), jnp.float32)] * 2,
        compiler_params=pltpu.CompilerParams(vmem_limit_bytes=16 * 1024 * 1024),
        cost_estimate=pl.CostEstimate(
            flops=10**9, bytes_accessed=100 * 10**6, transcendentals=0
        ),
    )(small)
    place1 = jnp.where(target % col_devices == my_col, target // col_devices, -1)
    place2 = jnp.where((target + 1) % col_devices == my_col, (target + 1) // col_devices, -1)
    scalars = jnp.stack(
        [
            my_row * height - first,
            place1,
            place2,
            target,
            my_col,
            jnp.int32(col_devices),
        ]
    ).astype(jnp.int32)
    return pl.pallas_call(
        finish_kernel,
        out_shape=jax.ShapeDtypeStruct((height, width), jnp.float32),
        in_specs=[pl.BlockSpec(memory_space=pltpu.SMEM)]
        + [pl.BlockSpec(memory_space=pltpu.VMEM)] * 4,
        out_specs=pl.BlockSpec(memory_space=pltpu.VMEM),
        compiler_params=pltpu.CompilerParams(vmem_limit_bytes=32 * 1024 * 1024),
    )(scalars, matrix, slab, bulk, factors)


def solution(mesh):
    return jax.shard_map(
        per_device,
        mesh=mesh,
        in_specs=(P("row", "col"), P()),
        out_specs=P("row", "col"),
        check_vma=False,
    )
```

```python
import jax
import jax.numpy as jnp
from jax import lax
from jax.experimental import pallas as pl
from jax.experimental.pallas import tpu as pltpu
from jax.sharding import PartitionSpec as P

NB = 128
SUB = 32
HI = lax.Precision.HIGHEST


def mm(a, b, ca=1, cb=0):
    return lax.dot_general(
        a, b, (((ca,), (cb,)), ((), ())), precision=HI, preferred_element_type=jnp.float32
    )


def eliminate(chains, m_ref, n_ref):
    count = len(chains)
    rows = lax.broadcasted_iota(jnp.int32, (NB, NB), 0)
    cols = lax.broadcasted_iota(jnp.int32, (NB, NB), 1)
    unit = (rows == cols).astype(jnp.float32)
    sub_row = lax.broadcasted_iota(jnp.int32, (SUB, 1), 0)
    for i, a in enumerate(chains):
        m_ref[i] = a
        n_ref[i] = unit
    pivots = [[] for _ in chains]
    for start in range(0, NB, SUB):
        m = [m_ref[i, start : start + SUB, :] for i in range(count)]
        n = [n_ref[i, start : start + SUB, :] for i in range(count)]
        inv = [jnp.zeros((SUB, 1), jnp.float32) for _ in range(count)]
        for j in range(SUB):
            c = start + j
            for i in range(count):
                recip = 1.0 / m[i][j : j + 1, c : c + 1]
                inv[i] = jnp.where(sub_row == j, recip, inv[i])
                if j < SUB - 1:
                    mult = jnp.where(sub_row > j, m[i][:, c : c + 1] * recip, 0.0)
                    m[i] = m[i] - mult * m[i][j : j + 1, :]
                    n[i] = n[i] - mult * n[i][j : j + 1, :]
        for i in range(count):
            n_ref[i, start : start + SUB, :] = n[i]
            pivots[i].append(inv[i])
        rest = start + SUB
        if rest < NB:
            for i in range(count):
                other = m[count - 1 - i] * inv[count - 1 - i]
                both = jnp.concatenate([m[i], n[i]], axis=1)
                change = mm(other, both, 0, 0)
                m_ref[i, rest:, :] -= change[rest:, :NB]
                n_ref[i, rest:, :] -= change[rest:, NB:]
    return [jnp.concatenate(p, axis=0) for p in pivots]


def factor_panel(gram, top, m_ref, n_ref):
    rows = lax.broadcasted_iota(jnp.int32, (NB, NB), 0)
    cols = lax.broadcasted_iota(jnp.int32, (NB, NB), 1)
    unit = (rows == cols).astype(jnp.float32)
    (inv,) = eliminate([gram], m_ref, n_ref)
    w = n_ref[0] * jnp.sqrt(inv)
    b = mm(top, w, 1, 1) + unit
    _, inv_t = eliminate([b, b.T], m_ref, n_ref)
    v = n_ref[1] * inv_t
    k = mm(v, n_ref[0], 0, 0)
    return w, b, k, v


def factor_kernel(small_ref, out_ref, m_ref, n_ref):
    g11 = small_ref[0:NB, 0:NB]
    g12 = small_ref[0:NB, NB:]
    g22 = small_ref[NB : 2 * NB, NB:]
    t11 = small_ref[2 * NB : 3 * NB, 0:NB]
    t12 = small_ref[2 * NB : 3 * NB, NB:]
    t21 = small_ref[3 * NB :, 0:NB]
    t22 = small_ref[3 * NB :, NB:]
    w1, b1, k1, v1 = factor_panel(g11 + mm(t11, t11, 0, 0), t11, m_ref, n_ref)
    x12 = mm(k1, mm(w1, g12) + mm(b1, t12, 0, 0))
    z = mm(w1, x12, 0, 0)
    g11z = mm(g11, z)
    zg = mm(z, g12, 0, 0)
    gram2 = g22 - zg - zg.T + mm(z, g11z, 0, 0)
    w2, b2, k2, v2 = factor_panel(gram2, t22 - mm(t21, z), m_ref, n_ref)
    for i, a in enumerate((w1, b1, k1, v1, z, w2, k2, v2, g12 - g11z, t21)):
        out_ref[i] = a


def gather_kernel(block_ref, out_ref, slots, send_sem, recv_sem):
    count = slots.shape[0]
    me = lax.axis_index("col")
    barrier = pltpu.get_barrier_semaphore()
    for k in range(1, count):
        pl.semaphore_signal(
            barrier,
            inc=1,
            device_id={"col": lax.rem(me + k, count)},
            device_id_type=pl.DeviceIdType.MESH,
        )
    pl.semaphore_wait(barrier, count - 1)
    copies = []
    for k in range(1, count):
        copy = pltpu.make_async_remote_copy(
            src_ref=block_ref,
            dst_ref=slots.at[me],
            send_sem=send_sem.at[k],
            recv_sem=recv_sem.at[k],
            device_id={"col": lax.rem(me + k, count)},
            device_id_type=pl.DeviceIdType.MESH,
        )
        copy.start()
        copies.append(copy)
    slots[me] = block_ref[...]
    for copy in copies:
        copy.wait_recv()
    out_ref[...] = slots[...]
    for copy in copies:
        copy.wait_send()


def prepare_kernel(s_ref, slots_ref, c_ref, slab_ref, part_ref, bulk_ref):
    height, width = c_ref.shape
    rel = lax.broadcasted_iota(jnp.int32, (height, 2 * NB), 0) + s_ref[0]
    slab_ref[:, 0:NB] = slots_ref[s_ref[5]]
    slab_ref[:, NB:] = slots_ref[s_ref[6]]
    below = jnp.where(rel >= NB, slab_ref[...], 0.0)
    part_ref[0 : 2 * NB, :] = mm(below, below, 0, 0)
    below_t = below.T
    step = 2 * NB

    def column(i, _):
        at = pl.ds(pl.multiple_of(i * step, step), step)
        bulk_ref[0 : 2 * NB, at] = mm(below_t, c_ref[:, at])
        return 0

    lax.fori_loop(0, width // step, column, 0)
    for i in range(2):
        at = pl.ds(pl.multiple_of(s_ref[1 + i], NB), NB)
        put = slice((2 + i) * NB, (3 + i) * NB)
        here = s_ref[3 + i] > 0
        part_ref[put, :] = jnp.where(here, slab_ref[at, :], 0.0)
        bulk_ref[put, :] = jnp.where(here, c_ref[at, :], 0.0)


def small_kernel(part, out_ref, arrived, total, send_sem, recv_sem, send_sem2, recv_sem2):
    count = arrived.shape[0]
    chunk = arrived.shape[1]
    me = lax.axis_index("row")
    peers = [lax.rem(me + k, count) for k in range(count)]
    barrier = pltpu.get_barrier_semaphore()
    for k in range(1, count):
        pl.semaphore_signal(
            barrier, inc=1, device_id={"row": peers[k]}, device_id_type=pl.DeviceIdType.MESH
        )
    pl.semaphore_wait(barrier, count - 1)

    def send(src, dst, k, sems):
        copy = pltpu.make_async_remote_copy(
            src_ref=src,
            dst_ref=dst,
            send_sem=sems[0].at[k],
            recv_sem=sems[1].at[k],
            device_id={"row": peers[k]},
            device_id_type=pl.DeviceIdType.MESH,
        )
        copy.start()
        return copy

    def rows_of(device):
        return pl.ds(pl.multiple_of(device * chunk, chunk), chunk)

    mine = rows_of(me)
    copies = [
        send(part.at[rows_of(peers[k])], arrived.at[k], k, (send_sem, recv_sem))
        for k in range(1, count)
    ]
    value = part[mine, :]
    for k in range(1, count):
        copies[k - 1].wait_recv()
        value = value + arrived[k]
    total[mine, :] = value
    again = [
        send(total.at[mine], total.at[mine], k, (send_sem2, recv_sem2)) for k in range(1, count)
    ]
    for copy in again:
        copy.wait_recv()
    out_ref[...] = total[...]
    for copy in copies + again:
        copy.wait_send()


def finish_kernel(s_ref, c_ref, a_ref, bulk_ref, fac_ref, out_ref):
    row_off = s_ref[0]
    place1, place2, target, my_col, col_devices = s_ref[1], s_ref[2], s_ref[3], s_ref[4], s_ref[5]
    height, width = c_ref.shape
    rel = lax.broadcasted_iota(jnp.int32, (height, NB), 0) + row_off
    diag = lax.broadcasted_iota(jnp.int32, (height, NB), 1)
    w1, b1, k1, v1, z, w2, k2, v2, h, t21 = [fac_ref[i] for i in range(10)]
    p1 = jnp.where(rel >= 0, a_ref[:, 0:NB], 0.0)
    full1 = mm(p1, w1, 1, 1) + (rel == diag).astype(jnp.float32)
    p2 = jnp.where(rel >= NB, a_ref[:, NB:] - mm(p1, z), 0.0)
    full2 = mm(p2, w2, 1, 1) + (rel == diag + NB).astype(jnp.float32)
    y1 = mm(full1, v1, 1, 1)
    y2 = mm(full2, v2, 1, 1)
    both = jnp.concatenate([full1, full2], axis=1)
    step = 2 * NB

    def column(i, _):
        at = pl.ds(pl.multiple_of(i * step, step), step)
        s1 = bulk_ref[0:NB, at]
        s2 = bulk_ref[NB : 2 * NB, at]
        top1 = bulk_ref[2 * NB : 3 * NB, at]
        top2 = bulk_ref[3 * NB :, at]
        block = (
            lax.broadcasted_iota(jnp.int32, (NB, step), 1) // NB + i * (step // NB)
        ) * col_devices + my_col
        x1 = mm(k1, mm(w1, s1) + mm(b1, top1, 0, 0))
        u1 = mm(w1, x1, 0, 0)
        x2 = mm(w2, s2 - mm(z, s1, 0, 0) - mm(h, u1, 0, 0)) + top2 - mm(t21, u1)
        x2 = mm(k2, x2)
        x1 = jnp.where(block > target, x1, 0.0)
        x2 = jnp.where(block > target + 1, x2, 0.0)
        out_ref[:, at] = c_ref[:, at] - mm(both, jnp.concatenate([x1, x2], axis=0))
        return 0

    lax.fori_loop(0, width // step, column, 0)

    @pl.when(place1 >= 0)
    def _():
        at = pl.ds(pl.multiple_of(place1 * NB, NB), NB)
        out_ref[:, at] = jnp.where(rel >= 0, y1, out_ref[:, at])

    @pl.when(place2 >= 0)
    def _():
        at = pl.ds(pl.multiple_of(place2 * NB, NB), NB)
        out_ref[:, at] = jnp.where(rel >= NB, y2, out_ref[:, at])


def per_device(matrix, panel_index):
    height, width = matrix.shape
    col_devices = lax.axis_size("col")
    my_row = lax.axis_index("row")
    my_col = lax.axis_index("col")
    target = panel_index[0]
    first = target * NB
    second = first + NB

    vmem = pl.BlockSpec(memory_space=pltpu.VMEM)
    smem = pl.BlockSpec(memory_space=pltpu.SMEM)
    owners = jnp.stack([target % col_devices, (target + 1) % col_devices]).astype(jnp.int32)
    held = jnp.where(owners[1] == my_col, target + 1, target) // col_devices
    candidate = lax.dynamic_slice_in_dim(matrix, held * NB, NB, 1)
    row_devices = lax.axis_size("row")
    chunk = 4 * NB // row_devices
    slots = pl.pallas_call(
        gather_kernel,
        out_shape=jax.ShapeDtypeStruct((col_devices, height, NB), jnp.float32),
        in_specs=[vmem],
        out_specs=vmem,
        scratch_shapes=[
            pltpu.VMEM((col_devices, height, NB), jnp.float32),
            pltpu.SemaphoreType.DMA((col_devices,)),
            pltpu.SemaphoreType.DMA((col_devices,)),
        ],
        compiler_params=pltpu.CompilerParams(
            collective_id=0, has_side_effects=True, vmem_limit_bytes=24 * 1024 * 1024
        ),
    )(candidate)
    tops = [first, second]
    places = jnp.stack(
        [my_row * height - first]
        + [at % height for at in tops]
        + [(at // height == my_row).astype(jnp.int32) for at in tops]
        + [owners[0], owners[1]]
    ).astype(jnp.int32)
    slab, part, bulk = pl.pallas_call(
        prepare_kernel,
        out_shape=[
            jax.ShapeDtypeStruct((height, 2 * NB), jnp.float32),
            jax.ShapeDtypeStruct((4 * NB, 2 * NB), jnp.float32),
            jax.ShapeDtypeStruct((4 * NB, width), jnp.float32),
        ],
        in_specs=[smem, vmem, vmem],
        out_specs=[vmem] * 3,
        compiler_params=pltpu.CompilerParams(vmem_limit_bytes=32 * 1024 * 1024),
    )(places, slots, matrix)
    bulk = lax.psum(bulk, "row")
    small = pl.pallas_call(
        small_kernel,
        out_shape=jax.ShapeDtypeStruct((4 * NB, 2 * NB), jnp.float32),
        in_specs=[vmem],
        out_specs=vmem,
        scratch_shapes=[
            pltpu.VMEM((row_devices, chunk, 2 * NB), jnp.float32),
            pltpu.VMEM((4 * NB, 2 * NB), jnp.float32),
        ]
        + [pltpu.SemaphoreType.DMA((row_devices,))] * 4,
        compiler_params=pltpu.CompilerParams(
            collective_id=1, has_side_effects=True, vmem_limit_bytes=16 * 1024 * 1024
        ),
        cost_estimate=pl.CostEstimate(
            flops=10**8, bytes_accessed=30 * 10**6, transcendentals=0
        ),
    )(part)
    factors = pl.pallas_call(
        factor_kernel,
        out_shape=jax.ShapeDtypeStruct((10, NB, NB), jnp.float32),
        in_specs=[pl.BlockSpec(memory_space=pltpu.VMEM)],
        out_specs=pl.BlockSpec(memory_space=pltpu.VMEM),
        scratch_shapes=[pltpu.VMEM((2, NB, NB), jnp.float32)] * 2,
        compiler_params=pltpu.CompilerParams(vmem_limit_bytes=16 * 1024 * 1024),
        cost_estimate=pl.CostEstimate(
            flops=10**9, bytes_accessed=100 * 10**6, transcendentals=0
        ),
    )(small)
    place1 = jnp.where(target % col_devices == my_col, target // col_devices, -1)
    place2 = jnp.where((target + 1) % col_devices == my_col, (target + 1) // col_devices, -1)
    scalars = jnp.stack(
        [
            my_row * height - first,
            place1,
            place2,
            target,
            my_col,
            jnp.int32(col_devices),
        ]
    ).astype(jnp.int32)
    return pl.pallas_call(
        finish_kernel,
        out_shape=jax.ShapeDtypeStruct((height, width), jnp.float32),
        in_specs=[pl.BlockSpec(memory_space=pltpu.SMEM)]
        + [pl.BlockSpec(memory_space=pltpu.VMEM)] * 4,
        out_specs=pl.BlockSpec(memory_space=pltpu.VMEM),
        compiler_params=pltpu.CompilerParams(vmem_limit_bytes=32 * 1024 * 1024),
    )(scalars, matrix, slab, bulk, factors)


def solution(mesh):
    return jax.shard_map(
        per_device,
        mesh=mesh,
        in_specs=(P("row", "col"), P()),
        out_specs=P("row", "col"),
        check_vma=False,
    )
```

```python
import jax
import jax.numpy as jnp
from jax import lax
from jax.experimental import pallas as pl
from jax.experimental.pallas import tpu as pltpu
from jax.sharding import PartitionSpec as P

NB = 128
SUB = 32
GROUP = 4
HI = lax.Precision.HIGHEST


def mm(a, b, ca=1, cb=0):
    return lax.dot_general(
        a, b, (((ca,), (cb,)), ((), ())), precision=HI, preferred_element_type=jnp.float32
    )


def eliminate(chains, m_ref, n_ref):
    count = len(chains)
    rows = lax.broadcasted_iota(jnp.int32, (NB, NB), 0)
    cols = lax.broadcasted_iota(jnp.int32, (NB, NB), 1)
    unit = (rows == cols).astype(jnp.float32)
    sub_row = lax.broadcasted_iota(jnp.int32, (SUB, NB), 0)
    for i, a in enumerate(chains):
        m_ref[i] = a
        n_ref[i] = unit
    pivots = [[] for _ in chains]
    for start in range(0, NB, SUB):
        m = [m_ref[i, start : start + SUB, :] for i in range(count)]
        n = [n_ref[i, start : start + SUB, :] for i in range(count)]
        inv = [jnp.zeros((SUB, NB), jnp.float32) for _ in range(count)]
        for j0 in range(0, SUB, GROUP):
            spread = [
                [
                    jnp.broadcast_to(m[i][:, start + j : start + j + 1], (SUB, NB))
                    for j in range(j0, j0 + GROUP)
                ]
                for i in range(count)
            ]
            for g in range(GROUP):
                j = j0 + g
                for i in range(count):
                    recip = 1.0 / spread[i][g][j : j + 1, :]
                    inv[i] = jnp.where(sub_row == j, recip, inv[i])
                    mult = jnp.where(sub_row > j, spread[i][g] * recip, 0.0)
                    for k in range(g + 1, GROUP):
                        spread[i][k] = spread[i][k] - mult * spread[i][k][j : j + 1, :]
                    m[i] = m[i] - mult * m[i][j : j + 1, :]
                    n[i] = n[i] - mult * n[i][j : j + 1, :]
        for i in range(count):
            n_ref[i, start : start + SUB, :] = n[i]
            pivots[i].append(inv[i])
        rest = start + SUB
        if rest < NB:
            for i in range(count):
                other = m[count - 1 - i] * inv[count - 1 - i]
                both = jnp.concatenate([m[i], n[i]], axis=1)
                change = mm(other, both, 0, 0)
                m_ref[i, rest:, :] -= change[rest:, :NB]
                n_ref[i, rest:, :] -= change[rest:, NB:]
    return [jnp.concatenate(p, axis=0) for p in pivots]


def factor_panel(gram, top, m_ref, n_ref):
    rows = lax.broadcasted_iota(jnp.int32, (NB, NB), 0)
    cols = lax.broadcasted_iota(jnp.int32, (NB, NB), 1)
    unit = (rows == cols).astype(jnp.float32)
    (inv,) = eliminate([gram], m_ref, n_ref)
    w = n_ref[0] * jnp.sqrt(inv)
    b = mm(top, w, 1, 1) + unit
    _, inv_t = eliminate([b, b.T], m_ref, n_ref)
    v = n_ref[1] * inv_t
    k = mm(v, n_ref[0], 0, 0)
    return w, b, k, v


def factor_kernel(small_ref, out_ref, m_ref, n_ref):
    g11 = small_ref[0:NB, 0:NB]
    g12 = small_ref[0:NB, NB:]
    g22 = small_ref[NB : 2 * NB, NB:]
    t11 = small_ref[2 * NB : 3 * NB, 0:NB]
    t12 = small_ref[2 * NB : 3 * NB, NB:]
    t21 = small_ref[3 * NB :, 0:NB]
    t22 = small_ref[3 * NB :, NB:]
    w1, b1, k1, v1 = factor_panel(g11 + mm(t11, t11, 0, 0), t11, m_ref, n_ref)
    x12 = mm(k1, mm(w1, g12) + mm(b1, t12, 0, 0))
    z = mm(w1, x12, 0, 0)
    g11z = mm(g11, z)
    zg = mm(z, g12, 0, 0)
    gram2 = g22 - zg - zg.T + mm(z, g11z, 0, 0)
    w2, b2, k2, v2 = factor_panel(gram2, t22 - mm(t21, z), m_ref, n_ref)
    for i, a in enumerate((w1, b1, k1, v1, z, w2, k2, v2, g12 - g11z, t21)):
        out_ref[i] = a


def gather_kernel(block_ref, out_ref, slots, send_sem, recv_sem):
    count = slots.shape[0]
    me = lax.axis_index("col")
    barrier = pltpu.get_barrier_semaphore()
    for k in range(1, count):
        pl.semaphore_signal(
            barrier,
            inc=1,
            device_id={"col": lax.rem(me + k, count)},
            device_id_type=pl.DeviceIdType.MESH,
        )
    pl.semaphore_wait(barrier, count - 1)
    copies = []
    for k in range(1, count):
        copy = pltpu.make_async_remote_copy(
            src_ref=block_ref,
            dst_ref=slots.at[me],
            send_sem=send_sem.at[k],
            recv_sem=recv_sem.at[k],
            device_id={"col": lax.rem(me + k, count)},
            device_id_type=pl.DeviceIdType.MESH,
        )
        copy.start()
        copies.append(copy)
    slots[me] = block_ref[...]
    for copy in copies:
        copy.wait_recv()
    out_ref[...] = slots[...]
    for copy in copies:
        copy.wait_send()


def prepare_kernel(s_ref, slots_ref, c_ref, slab_ref, part_ref, bulk_ref):
    height, width = c_ref.shape
    rel = lax.broadcasted_iota(jnp.int32, (height, 2 * NB), 0) + s_ref[0]
    slab_ref[:, 0:NB] = slots_ref[s_ref[5]]
    slab_ref[:, NB:] = slots_ref[s_ref[6]]
    below = jnp.where(rel >= NB, slab_ref[...], 0.0)
    part_ref[0 : 2 * NB, :] = mm(below, below, 0, 0)
    below_t = below.T
    step = 2 * NB

    def column(i, _):
        at = pl.ds(pl.multiple_of(i * step, step), step)
        bulk_ref[0 : 2 * NB, at] = mm(below_t, c_ref[:, at])
        return 0

    lax.fori_loop(0, width // step, column, 0)
    for i in range(2):
        at = pl.ds(pl.multiple_of(s_ref[1 + i], NB), NB)
        put = slice((2 + i) * NB, (3 + i) * NB)
        here = s_ref[3 + i] > 0
        part_ref[put, :] = jnp.where(here, slab_ref[at, :], 0.0)
        bulk_ref[put, :] = jnp.where(here, c_ref[at, :], 0.0)


def small_kernel(part, out_ref, arrived, total, send_sem, recv_sem, send_sem2, recv_sem2):
    count = arrived.shape[0]
    chunk = arrived.shape[1]
    me = lax.axis_index("row")
    peers = [lax.rem(me + k, count) for k in range(count)]
    barrier = pltpu.get_barrier_semaphore()
    for k in range(1, count):
        pl.semaphore_signal(
            barrier, inc=1, device_id={"row": peers[k]}, device_id_type=pl.DeviceIdType.MESH
        )
    pl.semaphore_wait(barrier, count - 1)

    def send(src, dst, k, sems):
        copy = pltpu.make_async_remote_copy(
            src_ref=src,
            dst_ref=dst,
            send_sem=sems[0].at[k],
            recv_sem=sems[1].at[k],
            device_id={"row": peers[k]},
            device_id_type=pl.DeviceIdType.MESH,
        )
        copy.start()
        return copy

    def rows_of(device):
        return pl.ds(pl.multiple_of(device * chunk, chunk), chunk)

    mine = rows_of(me)
    copies = [
        send(part.at[rows_of(peers[k])], arrived.at[k], k, (send_sem, recv_sem))
        for k in range(1, count)
    ]
    value = part[mine, :]
    for k in range(1, count):
        copies[k - 1].wait_recv()
        value = value + arrived[k]
    total[mine, :] = value
    again = [
        send(total.at[mine], total.at[mine], k, (send_sem2, recv_sem2)) for k in range(1, count)
    ]
    for copy in again:
        copy.wait_recv()
    out_ref[...] = total[...]
    for copy in copies + again:
        copy.wait_send()


def finish_kernel(s_ref, c_ref, a_ref, bulk_ref, fac_ref, out_ref):
    row_off = s_ref[0]
    place1, place2, target, my_col, col_devices = s_ref[1], s_ref[2], s_ref[3], s_ref[4], s_ref[5]
    height, width = c_ref.shape
    rel = lax.broadcasted_iota(jnp.int32, (height, NB), 0) + row_off
    diag = lax.broadcasted_iota(jnp.int32, (height, NB), 1)
    w1, b1, k1, v1, z, w2, k2, v2, h, t21 = [fac_ref[i] for i in range(10)]
    p1 = jnp.where(rel >= 0, a_ref[:, 0:NB], 0.0)
    full1 = mm(p1, w1, 1, 1) + (rel == diag).astype(jnp.float32)
    p2 = jnp.where(rel >= NB, a_ref[:, NB:] - mm(p1, z), 0.0)
    full2 = mm(p2, w2, 1, 1) + (rel == diag + NB).astype(jnp.float32)
    y1 = mm(full1, v1, 1, 1)
    y2 = mm(full2, v2, 1, 1)
    both = jnp.concatenate([full1, full2], axis=1)
    step = 2 * NB

    def column(i, _):
        at = pl.ds(pl.multiple_of(i * step, step), step)
        s1 = bulk_ref[0:NB, at]
        s2 = bulk_ref[NB : 2 * NB, at]
        top1 = bulk_ref[2 * NB : 3 * NB, at]
        top2 = bulk_ref[3 * NB :, at]
        block = (
            lax.broadcasted_iota(jnp.int32, (NB, step), 1) // NB + i * (step // NB)
        ) * col_devices + my_col
        x1 = mm(k1, mm(w1, s1) + mm(b1, top1, 0, 0))
        u1 = mm(w1, x1, 0, 0)
        x2 = mm(w2, s2 - mm(z, s1, 0, 0) - mm(h, u1, 0, 0)) + top2 - mm(t21, u1)
        x2 = mm(k2, x2)
        x1 = jnp.where(block > target, x1, 0.0)
        x2 = jnp.where(block > target + 1, x2, 0.0)
        out_ref[:, at] = c_ref[:, at] - mm(both, jnp.concatenate([x1, x2], axis=0))
        return 0

    lax.fori_loop(0, width // step, column, 0, unroll=True)

    @pl.when(place1 >= 0)
    def _():
        at = pl.ds(pl.multiple_of(place1 * NB, NB), NB)
        out_ref[:, at] = jnp.where(rel >= 0, y1, out_ref[:, at])

    @pl.when(place2 >= 0)
    def _():
        at = pl.ds(pl.multiple_of(place2 * NB, NB), NB)
        out_ref[:, at] = jnp.where(rel >= NB, y2, out_ref[:, at])


def per_device(matrix, panel_index):
    height, width = matrix.shape
    col_devices = lax.axis_size("col")
    my_row = lax.axis_index("row")
    my_col = lax.axis_index("col")
    target = panel_index[0]
    first = target * NB
    second = first + NB

    vmem = pl.BlockSpec(memory_space=pltpu.VMEM)
    smem = pl.BlockSpec(memory_space=pltpu.SMEM)
    owners = jnp.stack([target % col_devices, (target + 1) % col_devices]).astype(jnp.int32)
    held = jnp.where(owners[1] == my_col, target + 1, target) // col_devices
    candidate = lax.dynamic_slice_in_dim(matrix, held * NB, NB, 1)
    row_devices = lax.axis_size("row")
    chunk = 4 * NB // row_devices
    slots = pl.pallas_call(
        gather_kernel,
        out_shape=jax.ShapeDtypeStruct((col_devices, height, NB), jnp.float32),
        in_specs=[vmem],
        out_specs=vmem,
        scratch_shapes=[
            pltpu.VMEM((col_devices, height, NB), jnp.float32),
            pltpu.SemaphoreType.DMA((col_devices,)),
            pltpu.SemaphoreType.DMA((col_devices,)),
        ],
        compiler_params=pltpu.CompilerParams(
            collective_id=0, has_side_effects=True, vmem_limit_bytes=24 * 1024 * 1024
        ),
    )(candidate)
    tops = [first, second]
    places = jnp.stack(
        [my_row * height - first]
        + [at % height for at in tops]
        + [(at // height == my_row).astype(jnp.int32) for at in tops]
        + [owners[0], owners[1]]
    ).astype(jnp.int32)
    slab, part, bulk = pl.pallas_call(
        prepare_kernel,
        out_shape=[
            jax.ShapeDtypeStruct((height, 2 * NB), jnp.float32),
            jax.ShapeDtypeStruct((4 * NB, 2 * NB), jnp.float32),
            jax.ShapeDtypeStruct((4 * NB, width), jnp.float32),
        ],
        in_specs=[smem, vmem, vmem],
        out_specs=[vmem] * 3,
        compiler_params=pltpu.CompilerParams(vmem_limit_bytes=32 * 1024 * 1024),
    )(places, slots, matrix)
    bulk = lax.psum(bulk, "row")
    small = pl.pallas_call(
        small_kernel,
        out_shape=jax.ShapeDtypeStruct((4 * NB, 2 * NB), jnp.float32),
        in_specs=[vmem],
        out_specs=vmem,
        scratch_shapes=[
            pltpu.VMEM((row_devices, chunk, 2 * NB), jnp.float32),
            pltpu.VMEM((4 * NB, 2 * NB), jnp.float32),
        ]
        + [pltpu.SemaphoreType.DMA((row_devices,))] * 4,
        compiler_params=pltpu.CompilerParams(
            collective_id=1, has_side_effects=True, vmem_limit_bytes=16 * 1024 * 1024
        ),
        cost_estimate=pl.CostEstimate(
            flops=10**8, bytes_accessed=30 * 10**6, transcendentals=0
        ),
    )(part)
    factors = pl.pallas_call(
        factor_kernel,
        out_shape=jax.ShapeDtypeStruct((10, NB, NB), jnp.float32),
        in_specs=[pl.BlockSpec(memory_space=pltpu.VMEM)],
        out_specs=pl.BlockSpec(memory_space=pltpu.VMEM),
        scratch_shapes=[pltpu.VMEM((2, NB, NB), jnp.float32)] * 2,
        compiler_params=pltpu.CompilerParams(vmem_limit_bytes=16 * 1024 * 1024),
        cost_estimate=pl.CostEstimate(
            flops=10**9, bytes_accessed=100 * 10**6, transcendentals=0
        ),
    )(small)
    place1 = jnp.where(target % col_devices == my_col, target // col_devices, -1)
    place2 = jnp.where((target + 1) % col_devices == my_col, (target + 1) // col_devices, -1)
    scalars = jnp.stack(
        [
            my_row * height - first,
            place1,
            place2,
            target,
            my_col,
            jnp.int32(col_devices),
        ]
    ).astype(jnp.int32)
    return pl.pallas_call(
        finish_kernel,
        out_shape=jax.ShapeDtypeStruct((height, width), jnp.float32),
        in_specs=[pl.BlockSpec(memory_space=pltpu.SMEM)]
        + [pl.BlockSpec(memory_space=pltpu.VMEM)] * 4,
        out_specs=pl.BlockSpec(memory_space=pltpu.VMEM),
        compiler_params=pltpu.CompilerParams(vmem_limit_bytes=32 * 1024 * 1024),
    )(scalars, matrix, slab, bulk, factors)


def solution(mesh):
    return jax.shard_map(
        per_device,
        mesh=mesh,
        in_specs=(P("row", "col"), P()),
        out_specs=P("row", "col"),
        check_vma=False,
    )
```
